512 devices in a mesh: sec: 2 (over core), ep: 64 (over x, z), tp: 4 (over y).
Axes of the slice: x: 4, y: 4, z: 16, core: 2. Of those that a mesh axis runs over, the one named last changes fastest.
Arguments:
- tokens: bfloat16 [8192, 4096], P('ep', ('sec', 'tp')), may hold values from -6 to 6
- router_weight: bfloat16 [4096, 64], P(('sec', 'tp')), may hold values from -0.09375 to 0.09375
- expert_ids: int32 [8192, 8], P('ep'), may hold values from 0 to 63, all different within a row; in each aligned block of 128 rows (0 to 127, 128 to 255, ...) at most 20 rows name the same one
- gate_weight: bfloat16 [64, 4096, 1536], P('ep', 'sec', 'tp'), may hold values from -0.09375 to 0.09375
- up_weight: bfloat16 [64, 4096, 1536], P('ep', 'sec', 'tp'), may hold values from -0.09375 to 0.09375
- down_weight: bfloat16 [64, 1536, 4096], P('ep', None, ('sec', 'tp')), may hold values from -0.15625 to 0.15625
Outputs:
- mixture: bfloat16 [8192, 4096], P('ep', ('sec', 'tp'))
The draws below stay inside these ranges and needn't reach their ends.
Inputs may be any that keep to these rules, and one draw needn't show every extreme that they name: `expert_ids`: each row names 8 different experts. The 128 rows of one index of ep name no expert more than 20 times, a bound that some block reaches.
All inputs are finite; a program needn't handle non-finite values.
Results may differ from the reference program's by a relative error of at most 0.0057.
Values may be sent and summed in bfloat16 or wider, within the bound.
No kernel may reach another device: no remote copies, remote signals or barrier semaphores. Data moves between devices by JAX's collectives and lax.ppermute only.
A program may use at most 64 MiB of HBM per device.

```python
import math
import jax
import jax.numpy as jnp
import numpy as np
from jax import lax

D = 4096
EXPERTS = 64
FFW = 1536
TOP = 8
TOK_DEV = 128
CAP = 20
TOKENS = 8192
N_EP = 64


def shard_levels(key, dims, cuts, least, high):
    level, own = 1.0, jax.random.fold_in(key, 6)
    for dim, shards_of in cuts:
        heights = jnp.exp(jax.random.uniform(jax.random.fold_in(own, dim), (shards_of,), jnp.float32, least / len(cuts), high / len(cuts)))
        level = level * jnp.repeat(heights, dims[dim] // shards_of).reshape([-1 if axis == dim else 1 for axis in range(len(dims))])
    return level


def shared_out(own_key, own, number, rows, number_of, top, most, slope):
    order = jax.random.permutation(own_key, number_of)
    heavy_load, common = load_shares(number_of, rows * top, most, slope, True), load_shares(number_of, rows * top, most, slope, False)
    places = jnp.arange(number_of)

    def named(lengths, rotation):
        used = int((lengths > 0).sum())
        fixed = max(1, used // 4)
        passed = fixed + (places - fixed + rotation * (used - fixed)) % max(1, number_of - fixed)
        return jnp.zeros((number_of,), jnp.int32).at[order[jnp.where(places < fixed, places, passed)]].set(jnp.asarray(lengths, jnp.int32))

    lengths = jnp.where(number % 4 == 0, named(heavy_load, number // 4), named(common, number - number // 4 - 1))
    mixed = jax.random.permutation(jax.random.fold_in(own, 3), number_of)
    giver, receiver = mixed[0:number_of // 2 * 2:2], mixed[1:number_of // 2 * 2:2]
    room = jnp.minimum(lengths[giver] - 1, most - lengths[receiver]) // 2
    room = jnp.where((giver == order[0]) | (receiver == order[0]) | (lengths[receiver] == 0), 0, jnp.maximum(room, 0))
    passed = jax.random.randint(jax.random.fold_in(own, 4), (number_of // 2,), 0, 1 << 20) % (room + 1)
    lengths = lengths.at[giver].add(-passed).at[receiver].add(passed)
    members = jnp.searchsorted(jnp.cumsum(lengths), jnp.arange(rows * top), side="right").astype(jnp.int32)
    listing = members.reshape(top, rows).T
    listing = listing[jax.random.permutation(jax.random.fold_in(own, 1), rows)]
    rotation = jax.random.randint(jax.random.fold_in(own, 2), (rows, 1), 0, top)
    return jnp.take_along_axis(listing, (jnp.arange(top)[None, :] + rotation) % top, axis=1)


def load_shares(count, total, reach, lean, full):
    loads = [(1 << 20) // math.isqrt(rank ** lean) + 1 for rank in range(1, count + 1)]
    largest = reach if full else min(reach, max(-(-total // count), total * loads[0] // sum(loads)))
    least = 1 if total - largest >= count - 1 else 0
    holding, rest = [largest] + [least] * (count - 1), total - largest - least * (count - 1)
    while rest > 0:
        candidates = [i for i in range(1, count) if holding[i] < largest] or [i for i in range(1, count) if holding[i] < reach]
        pool, budget = sum([loads[i] for i in candidates]), rest
        for i in candidates:
            extra = min(reach - holding[i], max(1, budget * loads[i] // pool), rest)
            holding[i] = holding[i] + extra
            rest = rest - extra
    return np.array(holding)


def noise(rng, dims, width, bound, cuts=(), held_as=jnp.bfloat16):
    entries = jax.random.normal(rng, dims, jnp.float32) * width
    if len(cuts) > 0:
        entries = shard_levels(rng, dims, cuts, -0.22, 0.18) * entries
    return jnp.clip(entries, min=-bound, max=bound).astype(held_as)


def setup_inputs(seed: int = 0) -> dict:
    splits = jax.random.split(jax.random.key(seed), 7)
    tokens = noise(splits[0], (TOKENS, D), 1.0, 6.0, ((0, 64), (1, 8)))
    router_weight = noise(splits[1], (D, EXPERTS), D ** -0.5, 0.09375, ((0, 8),))
    expert_ids_keys = jax.random.split(jax.random.fold_in(splits[2], 1), TOKENS // TOK_DEV)
    expert_ids_turns = jax.random.permutation(jax.random.fold_in(splits[2], 3), TOKENS // TOK_DEV)
    expert_ids = jax.vmap(lambda own, number: shared_out(jax.random.fold_in(splits[2], 2), own, number, TOK_DEV, EXPERTS, TOP, CAP, 2))(expert_ids_keys, expert_ids_turns).reshape((TOKENS, TOP))
    gate_weight = noise(splits[3], (EXPERTS, D, FFW), D ** -0.5, 0.09375, ((0, 64), (1, 2), (2, 4)))
    up_weight = noise(splits[4], (EXPERTS, D, FFW), D ** -0.5, 0.09375, ((0, 64), (1, 2), (2, 4)))
    down_weight = noise(splits[5], (EXPERTS, FFW, D), FFW ** -0.5, 0.15625, ((0, 64), (2, 8)))
    return {"tokens": tokens, "router_weight": router_weight, "expert_ids": expert_ids, "gate_weight": gate_weight, "up_weight": up_weight, "down_weight": down_weight}


def reference(tokens, router_weight, expert_ids, gate_weight, up_weight, down_weight):
    logits = jnp.dot(tokens, router_weight, preferred_element_type=jnp.float32)
    picked = jnp.take_along_axis(logits, expert_ids, axis=1)
    raised = jnp.exp(picked)
    route_probs = raised / jnp.sum(raised, axis=1, keepdims=True)
    flat_ids = expert_ids.reshape(-1)
    flat_probs = route_probs.reshape(-1)
    slot_count = N_EP * CAP

    def one_expert(mix_acc, expert):
        matches = flat_ids == expert
        live_count = jnp.sum(matches.astype(jnp.int32))
        row_index = jnp.nonzero(matches, size=slot_count, fill_value=0)[0].astype(jnp.int32)
        live_slot = jnp.arange(slot_count, dtype=jnp.int32) < live_count
        tok_index = row_index // TOP
        picked_rows = tokens[tok_index]
        gate_acts = jnp.dot(picked_rows, gate_weight[expert], preferred_element_type=jnp.float32)
        up_acts = jnp.dot(picked_rows, up_weight[expert], preferred_element_type=jnp.float32)
        hidden = (jax.nn.silu(gate_acts) * up_acts).astype(jnp.bfloat16)
        expert_out = jnp.dot(hidden, down_weight[expert], preferred_element_type=jnp.float32).astype(jnp.bfloat16)
        row_scale = jnp.where(live_slot, flat_probs[row_index], jnp.zeros_like(flat_probs[row_index]))
        mix_acc = mix_acc.at[tok_index].add(row_scale[:, None] * expert_out.astype(jnp.float32))
        return mix_acc, None

    mix_acc, _ = lax.scan(one_expert, jnp.zeros((TOKENS, D), jnp.float32), jnp.arange(EXPERTS, dtype=jnp.int32))
    return mix_acc.astype(jnp.bfloat16)
```

```python
import jax
import jax.numpy as jnp
from jax import lax
from jax.sharding import PartitionSpec as P

EXPERTS = 64
CAP = 20
CHUNKS = 2
BF = jnp.bfloat16
F32 = jnp.float32


def shift(x, axis, size, by):
    return lax.ppermute(x, axis, [(i, (i + by) % size) for i in range(size)])


def ring_gather(x):
    half = x.shape[0] // 2
    behind = shift(x, "tp", 4, 1)
    ahead = shift(x, "tp", 4, -1)
    far_low = shift(behind[:half], "tp", 4, 1)
    far_high = shift(ahead[half:], "tp", 4, -1)
    return x, behind, far_low, far_high, ahead


def rolled(weight, me):
    rows = weight.shape[0] // 4
    parts = [lax.dynamic_slice_in_dim(weight, ((me - i) % 4) * rows, rows, 0) for i in range(4)]
    return jnp.concatenate(parts, axis=0)


def dot(a, b):
    return jnp.dot(a, b, preferred_element_type=F32)


def route(tokens, router_weight, expert_ids):
    rows = tokens.shape[0]
    chosen = jnp.any(expert_ids[:, :, None] == lax.broadcasted_iota(jnp.int32, (1, 1, EXPERTS), 2), axis=1)
    before = lax.broadcasted_iota(jnp.int32, (rows, rows), 0) > lax.broadcasted_iota(jnp.int32, (rows, rows), 1)
    rank = dot(before.astype(BF), chosen.astype(BF))
    slot = jnp.where(chosen, rank, F32(-1.0))
    return chosen, slot


def route_weights(tokens, router_weight, chosen):
    logits = dot(tokens, router_weight)
    logits = logits + shift(logits, "sec", 2, 1)
    logits = logits + shift(logits, "tp", 4, 1)
    logits = logits + shift(logits, "tp", 4, 2)
    raised = jnp.where(chosen, jnp.exp(logits), F32(0.0))
    return raised / jnp.sum(raised, axis=1, keepdims=True)


def per_device(tokens, router_weight, expert_ids, gate_weight, up_weight, down_weight):
    me = lax.axis_index("tp")
    sec = lax.axis_index("sec")
    width = tokens.shape[1]
    slots = CAP // CHUNKS
    rows = EXPERTS * slots
    pieces = width // 128
    gate_w, up_w, down_w = (rolled(w[0], me) for w in (gate_weight, up_weight, down_weight))

    chosen, slot = route(tokens, router_weight, expert_ids)
    column = lax.broadcasted_iota(jnp.int32, (1, rows), 1)
    spread = (lax.broadcasted_iota(jnp.int32, (EXPERTS, rows), 0) == column // slots).astype(BF)
    slot_wide = dot(slot.astype(BF), spread)
    picks = [slot_wide == (column % slots + c * slots).astype(F32) for c in range(CHUNKS)]

    arrived = []
    for pick in picks:
        outgoing = lax.dot_general(pick.astype(BF), tokens, (((0,), (0,)), ((), ())), preferred_element_type=F32).astype(BF)
        outgoing = outgoing.reshape(EXPERTS, slots * pieces, 128)
        arrived.append(lax.all_to_all(outgoing, "ep", split_axis=0, concat_axis=0, tiled=True))

    probs = route_weights(tokens, router_weight, chosen)
    probs_high = probs.astype(BF)
    probs_low = (probs - probs_high.astype(F32)).astype(BF)
    wide_high = dot(probs_high, spread).astype(BF)
    wide_low = dot(probs_low, spread).astype(BF)

    returned = []
    for block in arrived:
        own, behind, far_low, far_high, ahead = ring_gather(block)
        far = jnp.concatenate([far_low, far_high], axis=0)
        features = jnp.concatenate([b.reshape(rows, width) for b in (own, behind, far, ahead)], axis=1)
        acts = jnp.concatenate([dot(features, gate_w), dot(features, up_w)], axis=1)
        half = rows // 2
        kept = lax.dynamic_slice_in_dim(acts, sec * half, half, 0)
        sent = lax.dynamic_slice_in_dim(acts, (1 - sec) * half, half, 0).astype(BF)
        acts = kept + shift(sent, "sec", 2, 1).astype(F32)
        units = acts.shape[1] // 2
        hidden = (jax.nn.silu(acts[:, :units]) * acts[:, units:]).astype(BF)
        parts = ring_gather(hidden)
        others = [shift(p, "sec", 2, 1) for p in parts]
        outs = []
        for own, behind, far_low, far_high, ahead in (parts, others):
            far = jnp.concatenate([far_low, far_high], axis=0)
            outs.append(dot(jnp.concatenate([own, behind, far, ahead], axis=1), down_w).astype(BF))
        first = jnp.where(sec == 0, outs[0], outs[1])
        second = jnp.where(sec == 0, outs[1], outs[0])
        produced = jnp.concatenate([first, second], axis=0).reshape(EXPERTS, slots * pieces, 128)
        returned.append(lax.all_to_all(produced, "ep", split_axis=0, concat_axis=0, tiled=True))

    mixture = jnp.zeros(tokens.shape, F32)
    for pick, block in zip(picks, returned):
        block = block.reshape(rows, width)
        for wide in (wide_high, wide_low):
            mixture = mixture + dot(jnp.where(pick, wide, BF(0.0)), block)
    return mixture.astype(BF)


def solution(mesh):
    placed = (
        P("ep", ("sec", "tp")),
        P(("sec", "tp"), None),
        P("ep", None),
        P("ep", "sec", "tp"),
        P("ep", "sec", "tp"),
        P("ep", None, ("sec", "tp")),
    )
    return jax.shard_map(
        per_device, mesh=mesh, in_specs=placed, out_specs=P("ep", ("sec", "tp")), check_vma=False
    )
```

```python
import jax
import jax.numpy as jnp
from jax import lax
from jax.experimental import pallas as pl
from jax.experimental.pallas import tpu as pltpu
from jax.sharding import PartitionSpec as P

EXPERTS = 64
TOP = 8
SLOTS = 10
BF = jnp.bfloat16
F32 = jnp.float32
VMEM = pl.BlockSpec(memory_space=pltpu.VMEM)
SMEM = pl.BlockSpec(memory_space=pltpu.SMEM)


def call(body, outs, args, scalars=False, flops=0):
    specs = [SMEM if scalars and i == 0 else VMEM for i in range(len(args))]
    moved = sum(a.size * a.dtype.itemsize for a in args)
    return pl.pallas_call(
        body,
        out_shape=[jax.ShapeDtypeStruct(*o) for o in outs],
        in_specs=specs,
        out_specs=[VMEM] * len(outs),
        compiler_params=pltpu.CompilerParams(vmem_limit_bytes=44 << 20),
        cost_estimate=pl.CostEstimate(flops=flops, bytes_accessed=moved, transcendentals=0),
    )(*args)


def iota(shape, dim):
    return lax.broadcasted_iota(jnp.int32, shape, dim)


def ones_where(condition):
    return jnp.where(condition, F32(1.0), F32(0.0)).astype(BF)


def dot(a, b):
    return jnp.dot(a, b, preferred_element_type=F32)


def pack(extra):
    n = extra.shape[0]
    shape = (4 * n, n)
    total = jnp.zeros((4 * n, 128), F32)
    for f in range(4):
        total = total + dot(ones_where(iota(shape, 0) == 4 * iota(shape, 1) + f), extra[:, f * 128:(f + 1) * 128])
    return total.astype(BF)


def unpack(pieces):
    n = pieces.shape[0] // 4
    shape = (n, 4 * n)
    parts = [dot(ones_where(iota(shape, 1) == 4 * iota(shape, 0) + f), pieces).astype(BF) for f in range(4)]
    return jnp.concatenate(parts, axis=1)


def rows_of(half):
    return jnp.concatenate([half[:, :512], unpack(half[:, 512:])], axis=0)


def select_body(ids_ref, tokens_ref, a_ref, b_ref):
    ids = ids_ref[...]
    rows = tokens_ref.shape[0]
    shape = (EXPERTS, rows)
    chosen = jnp.zeros(shape, F32)
    for k in range(TOP):
        chosen = chosen + jnp.where(ids[k:k + 1, :] == iota(shape, 0), F32(1.0), F32(0.0))
    square = (rows, rows)
    rank = dot(chosen.astype(BF), ones_where(iota(square, 0) < iota(square, 1)))
    slot = jnp.where(chosen > 0, rank, F32(-1.0)).astype(BF)
    big, small = (EXPERTS * 8, EXPERTS), (EXPERTS * 2, EXPERTS)
    wide = dot(ones_where((iota(big, 0) >> 3) == iota(big, 1)), slot)
    wide2 = dot(ones_where((iota(small, 0) >> 1) == iota(small, 1)), slot)
    number = (iota(wide.shape, 0) & 7).astype(F32)
    number2 = (iota(wide2.shape, 0) & 1).astype(F32)
    tokens = tokens_ref[...]
    for c, ref in enumerate((a_ref, b_ref)):
        ref[:, :512] = dot(ones_where(wide == number + SLOTS * c), tokens).astype(BF)
        extra = dot(ones_where(wide2 == number2 + (SLOTS * c + 8)), tokens).astype(BF)
        ref[:, 512:] = pack(extra)


def near_body(place_ref, own_ref, b_lo, b_hi, a_lo, a_hi, gate_ref, up_ref, acc_ref):
    me = place_ref[0]
    for h in range(2):
        sources = (own_ref[h * 256:(h + 1) * 256, :], (b_lo, b_hi)[h][...], (a_lo, a_hi)[h][...])
        gate = jnp.zeros((320, 384), F32)
        up = jnp.zeros((320, 384), F32)
        for back, half in zip((0, 1, 3), sources):
            at = pl.ds(pl.multiple_of(((me + 4 - back) & 3) * 512, 512), 512)
            features = rows_of(half)
            gate = gate + dot(features, gate_ref[at, :])
            up = up + dot(features, up_ref[at, :])
        acc_ref[h * 320:(h + 1) * 320, :384] = gate
        acc_ref[h * 320:(h + 1) * 320, 384:] = up


def far_body(place_ref, lo, hi, acc_ref, gate_ref, up_ref, kept_ref, sent_ref):
    me = place_ref[0]
    first = place_ref[1] == 0
    at = pl.ds(pl.multiple_of(((me + 2) & 3) * 512, 512), 512)
    features = [rows_of(lo[...]), rows_of(hi[...])]
    for ref, columns in ((gate_ref, slice(0, 384)), (up_ref, slice(384, 768))):
        weight = ref[at, :]
        low = acc_ref[:320, columns] + dot(features[0], weight)
        high = acc_ref[320:, columns] + dot(features[1], weight)
        kept_ref[:, columns] = jnp.where(first, low, high)
        sent_ref[:, columns] = jnp.where(first, high, low).astype(BF)


def act_body(kept_ref, got_ref, hidden_ref):
    gate = kept_ref[:, :384] + got_ref[:, :384].astype(F32)
    up = kept_ref[:, 384:] + got_ref[:, 384:].astype(F32)
    hidden_ref[...] = (gate / (1.0 + jnp.exp(-gate)) * up).astype(BF)


def join_body(own, behind, far_lo, far_hi, ahead, full_ref):
    full_ref[:, :384] = own[...]
    full_ref[:, 384:768] = behind[...]
    full_ref[:160, 768:1152] = far_lo[...]
    full_ref[160:, 768:1152] = far_hi[...]
    full_ref[:, 1152:] = ahead[...]


def down_body(place_ref, full_ref, other_ref, down_ref, out_ref):
    me = place_ref[0]
    first = place_ref[1] == 0
    outs = []
    for ref in (full_ref, other_ref):
        total = jnp.zeros((320, 512), F32)
        for i in range(4):
            at = pl.ds(pl.multiple_of(((me + 4 - i) & 3) * 384, 384), 384)
            total = total + dot(ref[:, i * 384:(i + 1) * 384], down_ref[at, :])
        outs.append(total)
    ordered = (jnp.where(first, outs[0], outs[1]), jnp.where(first, outs[1], outs[0]))
    for h in range(2):
        rows = ordered[h].astype(BF)
        out_ref[h * 256:(h + 1) * 256, :512] = rows[:256]
        out_ref[h * 256:(h + 1) * 256, 512:] = pack(rows[256:])


def slots_of(ids):
    rows = ids.shape[0]
    shape = (rows, EXPERTS)
    chosen = jnp.zeros(shape, F32)
    for k in range(TOP):
        chosen = chosen + jnp.where(ids[:, k:k + 1] == iota(shape, 1), F32(1.0), F32(0.0))
    square = (rows, rows)
    rank = dot(ones_where(iota(square, 0) > iota(square, 1)), chosen.astype(BF))
    return chosen, jnp.where(chosen > 0, rank, F32(-1.0))


def weighted(slot, probs, block, c):
    slot = slot.astype(BF)
    high = probs.astype(BF)
    low = (probs - high.astype(F32)).astype(BF)
    total = jnp.zeros((slot.shape[0], 512), F32)
    for per, start, rows in ((8, 0, block[:, :512]), (2, 8, unpack(block[:, 512:]))):
        shape = (EXPERTS, EXPERTS * per)
        spread = ones_where((iota(shape, 1) >> (3 if per == 8 else 1)) == iota(shape, 0))
        wide = dot(slot, spread)
        number = (iota(wide.shape, 1) & (per - 1)).astype(F32) + (SLOTS * c + start)
        for part in (high, low):
            weight = jnp.where(wide == number, dot(part, spread), F32(0.0)).astype(BF)
            total = total + dot(weight, rows)
    return total


def combine_a_body(ids_ref, logits_ref, block_ref, acc_ref, probs_ref, slot_ref):
    chosen, slot = slots_of(ids_ref[...])
    raised = jnp.where(chosen > 0, jnp.exp(logits_ref[...]), F32(0.0))
    probs = raised / jnp.sum(raised, axis=1, keepdims=True)
    probs_ref[...] = probs
    slot_ref[...] = slot
    acc_ref[...] = weighted(slot, probs, block_ref[...], 0)


def combine_b_body(acc_ref, probs_ref, slot_ref, block_ref, out_ref):
    out_ref[...] = (acc_ref[...] + weighted(slot_ref[...], probs_ref[...], block_ref[...], 1)).astype(BF)


def shift(x, axis, size, by):
    return lax.ppermute(x, axis, [(i, (i + by) % size) for i in range(size)])


def exchange(x):
    return lax.all_to_all(x, "ep", split_axis=0, concat_axis=0, tiled=True)


def gather_features(block):
    lo, hi = block[:256], block[256:]
    b_lo = shift(lo, "tp", 4, 1)
    a_hi = shift(hi, "tp", 4, -1)
    b_hi = shift(hi, "tp", 4, 1)
    a_lo = shift(lo, "tp", 4, -1)
    return b_lo, b_hi, a_lo, a_hi, shift(b_lo, "tp", 4, 1), shift(a_hi, "tp", 4, -1)


def expand(place, block, gate_w, up_w):
    b_lo, b_hi, a_lo, a_hi, far_lo, far_hi = gather_features(block)
    acc, = call(near_body, [((640, 768), F32)], (place, block, b_lo, b_hi, a_lo, a_hi, gate_w, up_w), True, 3 << 29)
    kept, sent = call(
        far_body, [((320, 768), F32), ((320, 768), BF)], (place, far_lo, far_hi, acc, gate_w, up_w), True, 1 << 29
    )
    hidden, = call(act_body, [((320, 384), BF)], (kept, shift(sent, "sec", 2, 1)))
    return hidden


def contract(place, hidden, down_w):
    behind = shift(hidden, "tp", 4, 1)
    ahead = shift(hidden, "tp", 4, -1)
    far_lo = shift(behind[:160], "tp", 4, 1)
    far_hi = shift(ahead[160:], "tp", 4, -1)
    full, = call(join_body, [((320, 1536), BF)], (hidden, behind, far_lo, far_hi, ahead))
    produced, = call(down_body, [((512, 640), BF)], (place, full, shift(full, "sec", 2, 1), down_w), True, 1 << 30)
    return produced


def per_device(tokens, router_weight, expert_ids, gate_weight, up_weight, down_weight):
    place = jnp.stack([lax.axis_index("tp"), lax.axis_index("sec")]).astype(jnp.int32)
    gate_w, up_w, down_w = gate_weight[0], up_weight[0], down_weight[0]
    outgoing = call(select_body, [((512, 640), BF)] * 2, (expert_ids.T, tokens))
    block_a, block_b = exchange(outgoing[0]), exchange(outgoing[1])

    hidden_a = expand(place, block_a, gate_w, up_w)
    block_b, _ = lax.optimization_barrier((block_b, hidden_a))
    produced_a = contract(place, hidden_a, down_w)
    back_a = exchange(produced_a)
    hidden_b = expand(place, block_b, gate_w, up_w)
    produced_b = contract(place, hidden_b, down_w)
    produced_b, back_a = lax.optimization_barrier((produced_b, back_a))
    back_b = exchange(produced_b)

    logits = dot(tokens, router_weight)
    logits, _ = lax.optimization_barrier((logits, produced_b))
    logits = logits + shift(logits, "sec", 2, 1)
    logits = logits + shift(logits, "tp", 4, 1)
    logits = logits + shift(logits, "tp", 4, 2)
    table = ((128, EXPERTS), F32)
    acc, probs, slot = call(combine_a_body, [((128, 512), F32), table, table], (expert_ids, logits, back_a))
    mixture, = call(combine_b_body, [((128, 512), BF)], (acc, probs, slot, back_b))
    return mixture


def solution(mesh):
    placed = (
        P("ep", ("sec", "tp")),
        P(("sec", "tp"), None),
        P("ep", None),
        P("ep", "sec", "tp"),
        P("ep", "sec", "tp"),
        P("ep", None, ("sec", "tp")),
    )
    return jax.shard_map(
        per_device, mesh=mesh, in_specs=placed, out_specs=P("ep", ("sec", "tp")), check_vma=False
    )
```

```python
import functools

import jax
import jax.numpy as jnp
from jax import lax
from jax.experimental import pallas as pl
from jax.experimental.pallas import tpu as pltpu
from jax.sharding import PartitionSpec as P

EXPERTS = 64
TOP = 8
SLOTS = 10
BF = jnp.bfloat16
F32 = jnp.float32
VMEM = pl.BlockSpec(memory_space=pltpu.VMEM)
SMEM = pl.BlockSpec(memory_space=pltpu.SMEM)
HBM = pl.BlockSpec(memory_space=pltpu.HBM)


def call(body, outs, args, places=None, scratch=(), flops=0, aliases=None, out_places=None, limit=40):
    places = places or [VMEM] * len(args)
    moved = sum(a.size * a.dtype.itemsize for a in args)
    return pl.pallas_call(
        body,
        out_shape=[jax.ShapeDtypeStruct(*o) for o in outs],
        in_specs=places,
        out_specs=out_places or [VMEM] * len(outs),
        scratch_shapes=scratch,
        input_output_aliases=aliases or {},
        compiler_params=pltpu.CompilerParams(vmem_limit_bytes=limit << 20),
        cost_estimate=pl.CostEstimate(flops=flops, bytes_accessed=moved, transcendentals=0),
    )(*args)


def iota(shape, dim):
    return lax.broadcasted_iota(jnp.int32, shape, dim)


def ones_where(condition):
    return jnp.where(condition, F32(1.0), F32(0.0)).astype(BF)


def dot(a, b):
    return jnp.dot(a, b, preferred_element_type=F32)


def pack(extra):
    n = extra.shape[0]
    shape = (4 * n, n)
    total = jnp.zeros((4 * n, 128), F32)
    for f in range(4):
        total = total + dot(ones_where(iota(shape, 0) == 4 * iota(shape, 1) + f), extra[:, f * 128:(f + 1) * 128])
    return total.astype(BF)


def unpack(pieces):
    n = pieces.shape[0] // 4
    shape = (n, 4 * n)
    parts = [dot(ones_where(iota(shape, 1) == 4 * iota(shape, 0) + f), pieces).astype(BF) for f in range(4)]
    return jnp.concatenate(parts, axis=1)


def rows_of(half):
    return jnp.concatenate([half[:, :512], unpack(half[:, 512:])], axis=0)


def select_body(c, ids_ref, tokens_ref, out_ref, ids_at, tokens_at, sems):
    copies = [
        pltpu.make_async_copy(ids_ref, ids_at, sems.at[0]),
        pltpu.make_async_copy(tokens_ref, tokens_at, sems.at[1]),
    ]
    for copy in copies:
        copy.start()
    rows = tokens_at.shape[0]
    shape, square = (EXPERTS, rows), (rows, rows)
    big, small = (EXPERTS * 8, EXPERTS), (EXPERTS * 2, EXPERTS)
    spread = ones_where((iota(big, 0) >> 3) == iota(big, 1))
    spread2 = ones_where((iota(small, 0) >> 1) == iota(small, 1))
    before = ones_where(iota(square, 0) < iota(square, 1))
    copies[0].wait()
    ids = ids_at[...]
    chosen = jnp.zeros(shape, F32)
    for k in range(TOP):
        chosen = chosen + jnp.where(ids[k:k + 1, :] == iota(shape, 0), F32(1.0), F32(0.0))
    slot = jnp.where(chosen > 0, dot(chosen.astype(BF), before), F32(-1.0)).astype(BF)
    wide = dot(spread, slot)
    wide2 = dot(spread2, slot)
    number = (iota(wide.shape, 0) & 7).astype(F32) + SLOTS * c
    number2 = (iota(wide2.shape, 0) & 1).astype(F32) + (SLOTS * c + 8)
    copies[1].wait()
    tokens = tokens_at[...]
    out_ref[:, :512] = dot(ones_where(wide == number), tokens).astype(BF)
    out_ref[:, 512:] = pack(dot(ones_where(wide2 == number2), tokens).astype(BF))


def gate_up_body(place_ref, blocks_ref, gate_ref, up_ref, kept_ref, sent_ref, blocks_at, weights_at, total, sems):
    def copies(y):
        at = pl.ds(y * 512, 512)
        return (
            pltpu.make_async_copy(blocks_ref.at[at, :], blocks_at.at[at, :], sems.at[y, 0]),
            pltpu.make_async_copy(gate_ref.at[at, :], weights_at.at[at, pl.ds(0, 384)], sems.at[y, 1]),
            pltpu.make_async_copy(up_ref.at[at, :], weights_at.at[at, pl.ds(384, 384)], sems.at[y, 2]),
        )

    for y in range(2):
        for copy in copies(y):
            copy.start()
    first = place_ref[1] == 0
    for y in range(4):
        for copy in copies(y):
            copy.wait()
        if y < 2:
            for copy in copies(y + 2):
                copy.start()
        weights = weights_at[y * 512:(y + 1) * 512, :]
        sums = []
        for h in range(2):
            own = dot(rows_of(blocks_at[y * 512 + h * 256:y * 512 + (h + 1) * 256, :]), weights)
            sums.append(own if y == 0 else total[h * 320:(h + 1) * 320, :] + own)
        if y < 3:
            for h in range(2):
                total[h * 320:(h + 1) * 320, :] = sums[h]
        else:
            kept_ref[...] = jnp.where(first, sums[0], sums[1])
            sent_ref[...] = jnp.where(first, sums[1], sums[0]).astype(BF)


def act_body(kept_ref, got_ref, hidden_ref):
    gate = kept_ref[:, :384] + got_ref[:, :384].astype(F32)
    up = kept_ref[:, 384:] + got_ref[:, 384:].astype(F32)
    hidden_ref[...] = (gate / (1.0 + jnp.exp(-gate)) * up).astype(BF)


def down_half(side, hidden_ref, down_ref, out_ref, slab, sem):
    total = jnp.zeros((320, 512), F32)
    for y in range(4):
        total = total + dot(hidden_ref[y * 320:(y + 1) * 320, :], down_ref[y * 384:(y + 1) * 384, :])
    rows = total.astype(BF)
    slab[:, :512] = rows[:256]
    slab[:, 512:] = pack(rows[256:])
    copy = pltpu.make_async_copy(slab, out_ref.at[pl.ds(pl.multiple_of(side * 256, 256), 256), :], sem)
    copy.start()
    copy.wait()


def down_own_body(place_ref, hidden_ref, down_ref, out_ref, slab, sem):
    down_half(place_ref[1], hidden_ref, down_ref, out_ref, slab, sem)


def down_other_body(place_ref, hidden_ref, down_ref, own_ref, out_ref, slab, sem):
    down_half(1 - place_ref[1], hidden_ref, down_ref, out_ref, slab, sem)


def slots_of(ids):
    rows = ids.shape[0]
    shape = (rows, EXPERTS)
    chosen = jnp.zeros(shape, F32)
    for k in range(TOP):
        chosen = chosen + jnp.where(ids[:, k:k + 1] == iota(shape, 1), F32(1.0), F32(0.0))
    square = (rows, rows)
    rank = dot(ones_where(iota(square, 0) > iota(square, 1)), chosen.astype(BF))
    return chosen, jnp.where(chosen > 0, rank, F32(-1.0))


def weighted(slot, probs, block, c):
    slot = slot.astype(BF)
    high = probs.astype(BF)
    low = (probs - high.astype(F32)).astype(BF)
    total = jnp.zeros((slot.shape[0], 512), F32)
    for per, start, rows in ((8, 0, block[:, :512]), (2, 8, unpack(block[:, 512:]))):
        shape = (EXPERTS, EXPERTS * per)
        spread = ones_where((iota(shape, 1) >> (3 if per == 8 else 1)) == iota(shape, 0))
        wide = dot(slot, spread)
        number = (iota(wide.shape, 1) & (per - 1)).astype(F32) + (SLOTS * c + start)
        for part in (high, low):
            weight = jnp.where(wide == number, dot(part, spread), F32(0.0)).astype(BF)
            total = total + dot(weight, rows)
    return total


def combine_a_body(ids_ref, logits_ref, block_ref, acc_ref, probs_ref, slot_ref):
    chosen, slot = slots_of(ids_ref[...])
    raised = jnp.where(chosen > 0, jnp.exp(logits_ref[...]), F32(0.0))
    probs = raised / jnp.sum(raised, axis=1, keepdims=True)
    probs_ref[...] = probs
    slot_ref[...] = slot
    acc_ref[...] = weighted(slot, probs, block_ref[...], 0)


def combine_b_body(acc_ref, probs_ref, slot_ref, block_ref, out_ref):
    out_ref[...] = (acc_ref[...] + weighted(slot_ref[...], probs_ref[...], block_ref[...], 1)).astype(BF)


def shift(x, axis, size, by):
    return lax.ppermute(x, axis, [(i, (i + by) % size) for i in range(size)])


def exchange(x):
    return lax.all_to_all(x, "ep", split_axis=0, concat_axis=0, tiled=True)


def in_hbm(x):
    return pltpu.with_memory_space_constraint(x, pltpu.HBM)


def gate_up(place, blocks, gate_w, up_w):
    return call(
        gate_up_body,
        [((320, 768), F32), ((320, 768), BF)],
        (place, in_hbm(blocks), in_hbm(gate_w), in_hbm(up_w)),
        [SMEM, HBM, HBM, HBM],
        [
            pltpu.VMEM((2048, 640), BF),
            pltpu.VMEM((2048, 768), BF),
            pltpu.VMEM((640, 768), F32),
            pltpu.SemaphoreType.DMA((4, 3)),
        ],
        1 << 31,
    )


def activate(kept, sent):
    hidden, = call(act_body, [((320, 384), BF)], (kept, shift(sent, "sec", 2, 1)))
    return hidden


def contract(place, hidden, down_w):
    full = lax.all_gather(hidden, "tp", axis=0, tiled=True)
    other = shift(full, "sec", 2, 1)
    out = [((512, 640), BF)]
    scratch = [pltpu.VMEM((256, 640), BF), pltpu.SemaphoreType.DMA]
    own, = call(down_own_body, out, (place, full, down_w), [SMEM, VMEM, VMEM], scratch, 1 << 29, None, [HBM])
    produced, = call(
        down_other_body, out, (place, other, down_w, own), [SMEM, VMEM, VMEM, HBM], scratch, 1 << 29, {3: 0}, [HBM]
    )
    return produced


def per_device(tokens, router_weight, expert_ids, gate_weight, up_weight, down_weight):
    place = jnp.stack([lax.axis_index("tp"), lax.axis_index("sec")]).astype(jnp.int32)
    gate_w, up_w, down_w = gate_weight[0], up_weight[0], down_weight[0]
    names = expert_ids.T
    scratch = [pltpu.VMEM(names.shape, jnp.int32), pltpu.VMEM(tokens.shape, BF), pltpu.SemaphoreType.DMA((2,))]
    outgoing = [
        call(functools.partial(select_body, c), [((512, 640), BF)], (in_hbm(names), in_hbm(tokens)), [HBM, HBM], scratch)[0]
        for c in range(2)
    ]
    block_a = exchange(outgoing[0])
    block_a, slabs_b = lax.optimization_barrier((block_a, outgoing[1]))
    block_b = exchange(slabs_b)

    kept_a, sent_a = gate_up(place, lax.all_gather(block_a, "tp", axis=0, tiled=True), gate_w, up_w)
    block_b, _ = lax.optimization_barrier((block_b, sent_a))
    blocks_b = lax.all_gather(block_b, "tp", axis=0, tiled=True)
    produced_a = contract(place, activate(kept_a, sent_a), down_w)
    blocks_b, _ = lax.optimization_barrier((blocks_b, produced_a))
    back_a = exchange(produced_a)
    produced_b = contract(place, activate(*gate_up(place, blocks_b, gate_w, up_w)), down_w)
    produced_b, back_a = lax.optimization_barrier((produced_b, back_a))
    back_b = exchange(produced_b)

    logits = dot(tokens, router_weight)
    logits, _ = lax.optimization_barrier((logits, produced_b))
    logits = logits + shift(logits, "sec", 2, 1)
    logits = logits + shift(logits, "tp", 4, 1)
    logits = logits + shift(logits, "tp", 4, 2)
    table = ((128, EXPERTS), F32)
    acc, probs, slot = call(combine_a_body, [((128, 512), F32), table, table], (expert_ids, logits, back_a))
    mixture, = call(combine_b_body, [((128, 512), BF)], (acc, probs, slot, back_b))
    return mixture


def solution(mesh):
    placed = (
        P("ep", ("sec", "tp")),
        P(("sec", "tp"), None),
        P("ep", None),
        P("ep", "sec", "tp"),
        P("ep", "sec", "tp"),
        P("ep", None, ("sec", "tp")),
    )
    return jax.shard_map(
        per_device, mesh=mesh, in_specs=placed, out_specs=P("ep", ("sec", "tp")), check_vma=False
    )
```

```python
import functools

import jax
import jax.numpy as jnp
from jax import lax
from jax.experimental import pallas as pl
from jax.experimental.pallas import tpu as pltpu
from jax.sharding import PartitionSpec as P

EXPERTS = 64
TOP = 8
SLOTS = 10
BF = jnp.bfloat16
F32 = jnp.float32
VMEM = pl.BlockSpec(memory_space=pltpu.VMEM)
SMEM = pl.BlockSpec(memory_space=pltpu.SMEM)
HBM = pl.BlockSpec(memory_space=pltpu.HBM)


def call(body, outs, args, places=None, scratch=(), flops=0, aliases=None, out_places=None, limit=40):
    places = places or [VMEM] * len(args)
    moved = sum(a.size * a.dtype.itemsize for a in args)
    return pl.pallas_call(
        body,
        out_shape=[jax.ShapeDtypeStruct(*o) for o in outs],
        in_specs=places,
        out_specs=out_places or [VMEM] * len(outs),
        scratch_shapes=scratch,
        input_output_aliases=aliases or {},
        compiler_params=pltpu.CompilerParams(vmem_limit_bytes=limit << 20),
        cost_estimate=pl.CostEstimate(flops=flops, bytes_accessed=moved, transcendentals=0),
    )(*args)


def iota(shape, dim):
    return lax.broadcasted_iota(jnp.int32, shape, dim)


def ones_where(condition):
    return jnp.where(condition, F32(1.0), F32(0.0)).astype(BF)


def dot(a, b):
    return jnp.dot(a, b, preferred_element_type=F32)


def pack(extra):
    n = extra.shape[0]
    shape = (4 * n, n)
    total = jnp.zeros((4 * n, 128), F32)
    for f in range(4):
        total = total + dot(ones_where(iota(shape, 0) == 4 * iota(shape, 1) + f), extra[:, f * 128:(f + 1) * 128])
    return total.astype(BF)


def z_first(i):
    return ((i & 3) << 4) + (i >> 2)


def unpack(pieces):
    n = pieces.shape[0] // 4
    shape = (n, 4 * n)
    parts = [dot(ones_where(iota(shape, 1) == 4 * iota(shape, 0) + f), pieces).astype(BF) for f in range(4)]
    return jnp.concatenate(parts, axis=1)


def rows_of(half):
    return jnp.concatenate([half[:, :512], unpack(half[:, 512:])], axis=0)


def select_body(c, *refs):
    ids_ref, tokens_ref, out_ref, ids_at, tokens_at, sems = refs[c:]
    copies = [
        pltpu.make_async_copy(ids_ref, ids_at, sems.at[0]),
        pltpu.make_async_copy(tokens_ref, tokens_at, sems.at[1]),
    ]
    for copy in copies:
        copy.start()
    rows = tokens_at.shape[0]
    shape, square = (EXPERTS, rows), (rows, rows)
    big = (EXPERTS * 8, EXPERTS)

    def expert(i):
        if c == 0:
            return z_first(i)
        return ((((i >> 4) + refs[0][2]) & 3) << 4) + (i & 15)

    spread = ones_where(expert(iota(big, 0) >> 3) == iota(big, 1))
    before = ones_where(iota(square, 0) < iota(square, 1))
    copies[0].wait()
    ids = ids_at[...]
    chosen = jnp.zeros(shape, F32)
    for k in range(TOP):
        chosen = chosen + jnp.where(ids[k:k + 1, :] == iota(shape, 0), F32(1.0), F32(0.0))
    slot = jnp.where(chosen > 0, dot(chosen.astype(BF), before), F32(-1.0)).astype(BF)
    wide = dot(spread, slot)
    row = iota(wide.shape, 0) & 7
    main = ones_where(wide == (row + SLOTS * c).astype(F32))
    extra = wide == ((row >> 2) + (SLOTS * c + 8)).astype(F32)
    pieces = [ones_where(extra & ((row & 3) == f)) for f in range(4)]
    copies[1].wait()
    tokens = tokens_at[...]
    out_ref[:, :512] = dot(main, tokens).astype(BF)
    total = jnp.zeros((EXPERTS * 8, 128), F32)
    for f in range(4):
        total = total + dot(pieces[f], tokens[:, f * 128:(f + 1) * 128])
    out_ref[:, 512:] = total.astype(BF)


def gate_up_body(place_ref, blocks_ref, gate_ref, up_ref, kept_ref, sent_ref, blocks_at, weights_at, total, sems):
    def copies(y):
        at = pl.ds(y * 512, 512)
        return (
            pltpu.make_async_copy(blocks_ref.at[at, :], blocks_at.at[at, :], sems.at[y, 0]),
            pltpu.make_async_copy(gate_ref.at[at, :], weights_at.at[at, pl.ds(0, 384)], sems.at[y, 1]),
            pltpu.make_async_copy(up_ref.at[at, :], weights_at.at[at, pl.ds(384, 384)], sems.at[y, 2]),
        )

    for y in range(2):
        for copy in copies(y):
            copy.start()
    first = place_ref[1] == 0
    for y in range(4):
        for copy in copies(y):
            copy.wait()
        if y < 2:
            for copy in copies(y + 2):
                copy.start()
        weights = weights_at[y * 512:(y + 1) * 512, :]
        sums = []
        for h in range(2):
            own = dot(rows_of(blocks_at[y * 512 + h * 256:y * 512 + (h + 1) * 256, :]), weights)
            sums.append(own if y == 0 else total[h * 320:(h + 1) * 320, :] + own)
        if y < 3:
            for h in range(2):
                total[h * 320:(h + 1) * 320, :] = sums[h]
        else:
            kept_ref[...] = jnp.where(first, sums[0], sums[1])
            sent_ref[...] = jnp.where(first, sums[1], sums[0]).astype(BF)


def act_body(kept_ref, got_ref, hidden_ref):
    gate = kept_ref[:, :384] + got_ref[:, :384].astype(F32)
    up = kept_ref[:, 384:] + got_ref[:, 384:].astype(F32)
    hidden_ref[...] = (gate / (1.0 + jnp.exp(-gate)) * up).astype(BF)


def down_half(side, hidden_ref, down_ref, out_ref, slab, sem):
    total = jnp.zeros((320, 512), F32)
    for y in range(4):
        total = total + dot(hidden_ref[y * 320:(y + 1) * 320, :], down_ref[y * 384:(y + 1) * 384, :])
    rows = total.astype(BF)
    slab[:, :512] = rows[:256]
    slab[:, 512:] = pack(rows[256:])
    copy = pltpu.make_async_copy(slab, out_ref.at[pl.ds(pl.multiple_of(side * 256, 256), 256), :], sem)
    copy.start()
    copy.wait()


def down_own_body(place_ref, hidden_ref, down_ref, out_ref, slab, sem):
    down_half(place_ref[1], hidden_ref, down_ref, out_ref, slab, sem)


def down_other_body(place_ref, hidden_ref, down_ref, own_ref, out_ref, slab, sem):
    down_half(1 - place_ref[1], hidden_ref, down_ref, out_ref, slab, sem)


def slots_of(ids):
    rows = ids.shape[0]
    shape = (rows, EXPERTS)
    chosen = jnp.zeros(shape, F32)
    for k in range(TOP):
        chosen = chosen + jnp.where(ids[:, k:k + 1] == iota(shape, 1), F32(1.0), F32(0.0))
    square = (rows, rows)
    rank = dot(ones_where(iota(square, 0) > iota(square, 1)), chosen.astype(BF))
    return chosen, jnp.where(chosen > 0, rank, F32(-1.0))


def weighted(slot, probs, block, c, expert):
    high = probs.astype(BF)
    low = (probs - high.astype(F32)).astype(BF)
    shape = (EXPERTS, EXPERTS * 8)
    spread = ones_where(expert(iota(shape, 1) >> 3) == iota(shape, 0))
    wide = dot(slot.astype(BF), spread)
    row = iota(wide.shape, 1) & 7
    main = wide == (row + SLOTS * c).astype(F32)
    extra = wide == ((row >> 2) + (SLOTS * c + 8)).astype(F32)
    total = jnp.zeros((slot.shape[0], 512), F32)
    for part in (high, low):
        weight = dot(part, spread)
        total = total + dot(jnp.where(main, weight, F32(0.0)).astype(BF), block[:, :512])
        pieces = [
            dot(jnp.where(extra & ((row & 3) == f), weight, F32(0.0)).astype(BF), block[:, 512:]) for f in range(4)
        ]
        total = total + jnp.concatenate(pieces, axis=1)
    return total


def combine_a_body(place_ref, ids_ref, logits_ref, block_ref, acc_ref, probs_ref, slot_ref):
    chosen, slot = slots_of(ids_ref[...])
    raised = jnp.where(chosen > 0, jnp.exp(logits_ref[...]), F32(0.0))
    probs = raised / jnp.sum(raised, axis=1, keepdims=True)
    probs_ref[...] = probs
    slot_ref[...] = slot

    def expert(i):
        return (((place_ref[2] + 4 - (i >> 4)) & 3) << 4) + (i & 15)

    acc_ref[...] = weighted(slot, probs, block_ref[...], 0, expert)


def combine_b_body(acc_ref, probs_ref, slot_ref, block_ref, out_ref):
    out_ref[...] = (acc_ref[...] + weighted(slot_ref[...], probs_ref[...], block_ref[...], 1, z_first)).astype(BF)


def shift(x, axis, size, by):
    return lax.ppermute(x, axis, [(i, (i + by) % size) for i in range(size)])


def exchange(x, groups):
    return lax.all_to_all(x, "ep", split_axis=0, concat_axis=0, tiled=True, axis_index_groups=groups)


WHOLE = [[z_first(i) for i in range(64)]]
ALONG_Z = [[x * 16 + z for z in range(16)] for x in range(4)]


def shift_x(part, by):
    return lax.ppermute(part, "ep", [(i, (i + 16 * by) % 64) for i in range(64)])


def out_along_x(slabs, x):
    own, one, two, three = (slabs[d * 128:(d + 1) * 128] for d in range(4))
    parts = [own, shift_x(three, 3), shift_x(two, 2), shift_x(one, 1)]
    parts = jnp.stack([p.reshape(16, 8, 640) for p in parts + parts[:3]])
    parts = lax.dynamic_slice_in_dim(parts, (4 - x) & 3, 4, 0)
    return parts.transpose(1, 0, 2, 3).reshape(512, 640)


def back_along_x(slabs, x):
    slabs = slabs.reshape(16, 4, 8, 640)
    parts = []
    for d in range(4):
        part = lax.dynamic_slice_in_dim(slabs, (x + d) & 3, 1, 1).reshape(128, 640)
        parts.append(shift_x(part, d) if d else part)
    return jnp.concatenate(parts, axis=0)


def in_hbm(x):
    return pltpu.with_memory_space_constraint(x, pltpu.HBM)


def gate_up(place, blocks, gate_w, up_w):
    return call(
        gate_up_body,
        [((320, 768), F32), ((320, 768), BF)],
        (place, in_hbm(blocks), in_hbm(gate_w), in_hbm(up_w)),
        [SMEM, HBM, HBM, HBM],
        [
            pltpu.VMEM((2048, 640), BF),
            pltpu.VMEM((2048, 768), BF),
            pltpu.VMEM((640, 768), F32),
            pltpu.SemaphoreType.DMA((4, 3)),
        ],
        1 << 31,
    )


def activate(kept, sent):
    hidden, = call(act_body, [((320, 384), BF)], (kept, shift(sent, "sec", 2, 1)))
    return hidden


def gather(hidden):
    return lax.all_gather(hidden, "tp", axis=0, tiled=True)


def contract(place, full, down_w):
    other = shift(full, "sec", 2, 1)
    out = [((512, 640), BF)]
    scratch = [pltpu.VMEM((256, 640), BF), pltpu.SemaphoreType.DMA]
    own, = call(down_own_body, out, (place, full, down_w), [SMEM, VMEM, VMEM], scratch, 1 << 29, None, [HBM])
    produced, = call(
        down_other_body, out, (place, other, down_w, own), [SMEM, VMEM, VMEM, HBM], scratch, 1 << 29, {3: 0}, [HBM]
    )
    return produced


def per_device(tokens, router_weight, expert_ids, gate_weight, up_weight, down_weight):
    x = (lax.axis_index("ep") >> 4).astype(jnp.int32)
    place = jnp.stack([lax.axis_index("tp"), lax.axis_index("sec"), x]).astype(jnp.int32)
    gate_w, up_w, down_w = gate_weight[0], up_weight[0], down_weight[0]
    names = expert_ids.T
    scratch = [pltpu.VMEM(names.shape, jnp.int32), pltpu.VMEM(tokens.shape, BF), pltpu.SemaphoreType.DMA((2,))]
    sources = (in_hbm(names), in_hbm(tokens))
    out = [((512, 640), BF)]
    slabs_a, = call(functools.partial(select_body, 0), out, sources, [HBM, HBM], scratch)
    slabs_b, = call(functools.partial(select_body, 1), out, (place, *sources), [SMEM, HBM, HBM], scratch)
    block_a = exchange(slabs_a, WHOLE)
    slabs_b = out_along_x(slabs_b, x)
    block_a, slabs_b = lax.optimization_barrier((block_a, slabs_b))
    block_b = exchange(slabs_b, ALONG_Z)

    blocks_a = lax.all_gather(block_a, "tp", axis=0, tiled=True)
    blocks_a, block_b = lax.optimization_barrier((blocks_a, block_b))
    kept_a, sent_a = gate_up(place, blocks_a, gate_w, up_w)
    blocks_b = lax.all_gather(block_b, "tp", axis=0, tiled=True)
    produced_a = contract(place, gather(activate(kept_a, sent_a)), down_w)
    blocks_b, _ = lax.optimization_barrier((blocks_b, produced_a))
    back_a = exchange(produced_a, ALONG_Z)
    produced_b = contract(place, gather(activate(*gate_up(place, blocks_b, gate_w, up_w))), down_w)
    produced_b, back_a = lax.optimization_barrier((produced_b, back_a))
    back_b = exchange(produced_b, WHOLE)
    back_a = back_along_x(back_a, x)

    logits = dot(tokens, router_weight)
    logits, _ = lax.optimization_barrier((logits, produced_b))
    logits = logits + shift(logits, "sec", 2, 1)
    logits = logits + shift(logits, "tp", 4, 1)
    logits = logits + shift(logits, "tp", 4, 2)
    table = ((128, EXPERTS), F32)
    acc, probs, slot = call(combine_a_body, [((128, 512), F32), table, table], (place, expert_ids, logits, back_a), [SMEM] + [VMEM] * 3)
    mixture, = call(combine_b_body, [((128, 512), BF)], (acc, probs, slot, back_b))
    return mixture


def solution(mesh):
    placed = (
        P("ep", ("sec", "tp")),
        P(("sec", "tp"), None),
        P("ep", None),
        P("ep", "sec", "tp"),
        P("ep", "sec", "tp"),
        P("ep", None, ("sec", "tp")),
    )
    return jax.shard_map(
        per_device, mesh=mesh, in_specs=placed, out_specs=P("ep", ("sec", "tp")), check_vma=False
    )
```

```python
import functools

import jax
import jax.numpy as jnp
from jax import lax
from jax.experimental import pallas as pl
from jax.experimental.pallas import tpu as pltpu
from jax.sharding import PartitionSpec as P

EXPERTS = 64
TOP = 8
SLOTS = 10
BF = jnp.bfloat16
F32 = jnp.float32
VMEM = pl.BlockSpec(memory_space=pltpu.VMEM)
SMEM = pl.BlockSpec(memory_space=pltpu.SMEM)
HBM = pl.BlockSpec(memory_space=pltpu.HBM)


def call(body, outs, args, places=None, scratch=(), flops=0, aliases=None, out_places=None, limit=40):
    places = places or [VMEM] * len(args)
    moved = sum(a.size * a.dtype.itemsize for a in args)
    return pl.pallas_call(
        body,
        out_shape=[jax.ShapeDtypeStruct(*o) for o in outs],
        in_specs=places,
        out_specs=out_places or [VMEM] * len(outs),
        scratch_shapes=scratch,
        input_output_aliases=aliases or {},
        compiler_params=pltpu.CompilerParams(vmem_limit_bytes=limit << 20),
        cost_estimate=pl.CostEstimate(flops=flops, bytes_accessed=moved, transcendentals=0),
    )(*args)


def iota(shape, dim):
    return lax.broadcasted_iota(jnp.int32, shape, dim)


def ones_where(condition):
    return jnp.where(condition, F32(1.0), F32(0.0)).astype(BF)


def dot(a, b):
    return jnp.dot(a, b, preferred_element_type=F32)


def pack(extra):
    n = extra.shape[0]
    shape = (4 * n, n)
    total = jnp.zeros((4 * n, 128), F32)
    for f in range(4):
        total = total + dot(ones_where(iota(shape, 0) == 4 * iota(shape, 1) + f), extra[:, f * 128:(f + 1) * 128])
    return total.astype(BF)


def z_first(i):
    return ((i & 3) << 4) + (i >> 2)


def unpack(pieces):
    n = pieces.shape[0] // 4
    shape = (n, 4 * n)
    parts = [dot(ones_where(iota(shape, 1) == 4 * iota(shape, 0) + f), pieces).astype(BF) for f in range(4)]
    return jnp.concatenate(parts, axis=1)


def rows_of(half):
    return jnp.concatenate([half[:, :512], unpack(half[:, 512:])], axis=0)


def select_body(c, *refs):
    ids_ref, tokens_ref, out_ref, ids_at, tokens_at, sems = refs[c:]
    copies = [
        pltpu.make_async_copy(ids_ref, ids_at, sems.at[0]),
        pltpu.make_async_copy(tokens_ref, tokens_at, sems.at[1]),
    ]
    for copy in copies:
        copy.start()
    rows = tokens_at.shape[0]
    shape, square = (EXPERTS, rows), (rows, rows)
    big = (EXPERTS * 8, EXPERTS)

    def expert(i):
        if c == 0:
            return z_first(i)
        return ((((i >> 4) + refs[0][2]) & 3) << 4) + (i & 15)

    spread = ones_where(expert(iota(big, 0) >> 3) == iota(big, 1))
    before = ones_where(iota(square, 0) < iota(square, 1))
    copies[0].wait()
    ids = ids_at[...]
    chosen = jnp.zeros(shape, F32)
    for k in range(TOP):
        chosen = chosen + jnp.where(ids[k:k + 1, :] == iota(shape, 0), F32(1.0), F32(0.0))
    slot = jnp.where(chosen > 0, dot(chosen.astype(BF), before), F32(-1.0)).astype(BF)
    wide = dot(spread, slot)
    row = iota(wide.shape, 0) & 7
    main = ones_where(wide == (row + SLOTS * c).astype(F32))
    extra = wide == ((row >> 2) + (SLOTS * c + 8)).astype(F32)
    pieces = [ones_where(extra & ((row & 3) == f)) for f in range(4)]
    copies[1].wait()
    tokens = tokens_at[...]
    out_ref[:, :512] = dot(main, tokens).astype(BF)
    total = jnp.zeros((EXPERTS * 8, 128), F32)
    for f in range(4):
        total = total + dot(pieces[f], tokens[:, f * 128:(f + 1) * 128])
    out_ref[:, 512:] = total.astype(BF)


def gate_up_body(place_ref, blocks_ref, gate_ref, up_ref, kept_ref, sent_ref, blocks_at, weights_at, total, sems):
    def copies(y):
        at = pl.ds(y * 512, 512)
        return (
            pltpu.make_async_copy(blocks_ref.at[at, :], blocks_at.at[at, :], sems.at[y, 0]),
            pltpu.make_async_copy(gate_ref.at[at, :], weights_at.at[at, pl.ds(0, 384)], sems.at[y, 1]),
            pltpu.make_async_copy(up_ref.at[at, :], weights_at.at[at, pl.ds(384, 384)], sems.at[y, 2]),
        )

    for y in range(2):
        for copy in copies(y):
            copy.start()
    first = place_ref[1] == 0
    for y in range(4):
        for copy in copies(y):
            copy.wait()
        if y < 2:
            for copy in copies(y + 2):
                copy.start()
        weights = weights_at[y * 512:(y + 1) * 512, :]
        sums = []
        for h in range(2):
            own = dot(rows_of(blocks_at[y * 512 + h * 256:y * 512 + (h + 1) * 256, :]), weights)
            sums.append(own if y == 0 else total[h * 320:(h + 1) * 320, :] + own)
        if y < 3:
            for h in range(2):
                total[h * 320:(h + 1) * 320, :] = sums[h]
        else:
            kept_ref[...] = jnp.where(first, sums[0], sums[1])
            sent_ref[...] = jnp.where(first, sums[1], sums[0]).astype(BF)


def act_body(kept_ref, got_ref, hidden_ref):
    gate = kept_ref[:, :384] + got_ref[:, :384].astype(F32)
    up = kept_ref[:, 384:] + got_ref[:, 384:].astype(F32)
    hidden_ref[...] = (gate / (1.0 + jnp.exp(-gate)) * up).astype(BF)


def down_half(side, hidden_ref, down_ref, out_ref, slab, sem):
    units = jnp.concatenate([hidden_ref[y * 320:(y + 1) * 320, :] for y in range(4)], axis=1)
    total = dot(units, down_ref[...])
    rows = total.astype(BF)
    slab[:, :512] = rows[:256]
    slab[:, 512:] = pack(rows[256:])
    copy = pltpu.make_async_copy(slab, out_ref.at[pl.ds(pl.multiple_of(side * 256, 256), 256), :], sem)
    copy.start()
    copy.wait()


def down_own_body(place_ref, hidden_ref, down_ref, out_ref, slab, sem):
    down_half(place_ref[1], hidden_ref, down_ref, out_ref, slab, sem)


def down_other_body(place_ref, hidden_ref, down_ref, own_ref, out_ref, slab, sem):
    down_half(1 - place_ref[1], hidden_ref, down_ref, out_ref, slab, sem)


def slots_of(ids):
    rows = ids.shape[0]
    shape = (rows, EXPERTS)
    chosen = jnp.zeros(shape, F32)
    for k in range(TOP):
        chosen = chosen + jnp.where(ids[:, k:k + 1] == iota(shape, 1), F32(1.0), F32(0.0))
    square = (rows, rows)
    rank = dot(ones_where(iota(square, 0) > iota(square, 1)), chosen.astype(BF))
    return chosen, jnp.where(chosen > 0, rank, F32(-1.0))


def weights_of(slot, probs, c, expert):
    high = probs.astype(BF)
    low = (probs - high.astype(F32)).astype(BF)
    shape = (EXPERTS, EXPERTS * 8)
    spread = ones_where(expert(iota(shape, 1) >> 3) == iota(shape, 0))
    wide = dot(slot.astype(BF), spread)
    row = iota(wide.shape, 1) & 7
    main = wide == (row + SLOTS * c).astype(F32)
    extra = wide == ((row >> 2) + (SLOTS * c + 8)).astype(F32)
    parts = [dot(part, spread) for part in (high, low)]
    masks = [main] + [extra & ((row & 3) == f) for f in range(4)]
    return [jnp.where(mask, part, F32(0.0)).astype(BF) for mask in masks for part in parts]


def weighted(weights, block):
    n = weights.shape[0] // 10
    main = dot(weights[:2 * n], block[:, :512])
    extra = dot(weights[2 * n:], block[:, 512:])
    pieces = [extra[2 * f * n:(2 * f + 1) * n] + extra[(2 * f + 1) * n:(2 * f + 2) * n] for f in range(4)]
    return main[:n] + main[n:] + jnp.concatenate(pieces, axis=1)


def combine_a_body(place_ref, ids_ref, logits_ref, block_ref, acc_ref, weights_ref):
    chosen, slot = slots_of(ids_ref[...])
    raised = jnp.where(chosen > 0, jnp.exp(logits_ref[...]), F32(0.0))
    probs = raised / jnp.sum(raised, axis=1, keepdims=True)

    def expert(i):
        return (((place_ref[2] + 4 - (i >> 4)) & 3) << 4) + (i & 15)

    acc_ref[...] = weighted(jnp.concatenate(weights_of(slot, probs, 0, expert), axis=0), block_ref[...])
    for i, part in enumerate(weights_of(slot, probs, 1, z_first)):
        weights_ref[i * 128:(i + 1) * 128, :] = part


def combine_b_body(acc_ref, weights_ref, block_ref, out_ref):
    out_ref[...] = (acc_ref[...] + weighted(weights_ref[...], block_ref[...])).astype(BF)


def shift(x, axis, size, by):
    return lax.ppermute(x, axis, [(i, (i + by) % size) for i in range(size)])


def exchange(x, groups):
    return lax.all_to_all(x, "ep", split_axis=0, concat_axis=0, tiled=True, axis_index_groups=groups)


WHOLE = [[z_first(i) for i in range(64)]]
ALONG_Z = [[x * 16 + z for z in range(16)] for x in range(4)]


def shift_x(part, by):
    return lax.ppermute(part, "ep", [(i, (i + 16 * by) % 64) for i in range(64)])


def out_along_x(slabs, x):
    own, one, two, three = (slabs[d * 128:(d + 1) * 128] for d in range(4))
    parts = [own, shift_x(three, 3), shift_x(two, 2), shift_x(one, 1)]
    parts = jnp.stack([p.reshape(16, 8, 640) for p in parts + parts[:3]])
    parts = lax.dynamic_slice_in_dim(parts, (4 - x) & 3, 4, 0)
    return parts.transpose(1, 0, 2, 3).reshape(512, 640)


def back_along_x(slabs, x):
    slabs = slabs.reshape(16, 4, 8, 640)
    parts = []
    for d in range(4):
        part = lax.dynamic_slice_in_dim(slabs, (x + d) & 3, 1, 1).reshape(128, 640)
        parts.append(shift_x(part, d) if d else part)
    return jnp.concatenate(parts, axis=0)


def in_hbm(x):
    return pltpu.with_memory_space_constraint(x, pltpu.HBM)


def gate_up(place, blocks, gate_w, up_w):
    return call(
        gate_up_body,
        [((320, 768), F32), ((320, 768), BF)],
        (place, in_hbm(blocks), in_hbm(gate_w), in_hbm(up_w)),
        [SMEM, HBM, HBM, HBM],
        [
            pltpu.VMEM((2048, 640), BF),
            pltpu.VMEM((2048, 768), BF),
            pltpu.VMEM((640, 768), F32),
            pltpu.SemaphoreType.DMA((4, 3)),
        ],
        1 << 31,
    )


def activate(kept, sent):
    hidden, = call(act_body, [((320, 384), BF)], (kept, shift(sent, "sec", 2, 1)))
    return hidden


def gather(hidden):
    return lax.all_gather(hidden, "tp", axis=0, tiled=True)


def contract(place, full, down_w):
    other = shift(full, "sec", 2, 1)
    out = [((512, 640), BF)]
    scratch = [pltpu.VMEM((256, 640), BF), pltpu.SemaphoreType.DMA]
    own, = call(down_own_body, out, (place, full, down_w), [SMEM, VMEM, VMEM], scratch, 1 << 29, None, [HBM])
    produced, = call(
        down_other_body, out, (place, other, down_w, own), [SMEM, VMEM, VMEM, HBM], scratch, 1 << 29, {3: 0}, [HBM]
    )
    return produced


def per_device(tokens, router_weight, expert_ids, gate_weight, up_weight, down_weight):
    x = (lax.axis_index("ep") >> 4).astype(jnp.int32)
    place = jnp.stack([lax.axis_index("tp"), lax.axis_index("sec"), x]).astype(jnp.int32)
    gate_w, up_w, down_w = gate_weight[0], up_weight[0], down_weight[0]
    names = expert_ids.T
    scratch = [pltpu.VMEM(names.shape, jnp.int32), pltpu.VMEM(tokens.shape, BF), pltpu.SemaphoreType.DMA((2,))]
    sources = (in_hbm(names), in_hbm(tokens))
    out = [((512, 640), BF)]
    slabs_a, = call(functools.partial(select_body, 0), out, sources, [HBM, HBM], scratch)
    slabs_b, = call(functools.partial(select_body, 1), out, (place, *sources), [SMEM, HBM, HBM], scratch)
    block_a = exchange(slabs_a, WHOLE)
    slabs_b = out_along_x(slabs_b, x)
    block_a, slabs_b = lax.optimization_barrier((block_a, slabs_b))
    block_b = exchange(slabs_b, ALONG_Z)

    blocks_a = lax.all_gather(block_a, "tp", axis=0, tiled=True)
    blocks_a, block_b = lax.optimization_barrier((blocks_a, block_b))
    kept_a, sent_a = gate_up(place, blocks_a, gate_w, up_w)
    blocks_b = lax.all_gather(block_b, "tp", axis=0, tiled=True)
    produced_a = contract(place, gather(activate(kept_a, sent_a)), down_w)
    blocks_b, _ = lax.optimization_barrier((blocks_b, produced_a))
    back_a = exchange(produced_a, ALONG_Z)
    produced_b = contract(place, gather(activate(*gate_up(place, blocks_b, gate_w, up_w))), down_w)
    produced_b, back_a = lax.optimization_barrier((produced_b, back_a))
    back_b = exchange(produced_b, WHOLE)
    back_a = back_along_x(back_a, x)

    logits = dot(tokens, router_weight)
    logits, _ = lax.optimization_barrier((logits, produced_b))
    logits = logits + shift(logits, "sec", 2, 1)
    logits = logits + shift(logits, "tp", 4, 1)
    logits = logits + shift(logits, "tp", 4, 2)
    acc, weights_b = call(
        combine_a_body,
        [((128, 512), F32), ((1280, 512), BF)],
        (place, expert_ids, logits, back_a),
        [SMEM] + [VMEM] * 3,
    )
    mixture, = call(combine_b_body, [((128, 512), BF)], (acc, weights_b, back_b))
    return mixture


def solution(mesh):
    placed = (
        P("ep", ("sec", "tp")),
        P(("sec", "tp"), None),
        P("ep", None),
        P("ep", "sec", "tp"),
        P("ep", "sec", "tp"),
        P("ep", None, ("sec", "tp")),
    )
    return jax.shard_map(
        per_device, mesh=mesh, in_specs=placed, out_specs=P("ep", ("sec", "tp")), check_vma=False
    )
```

```python
import functools

import jax
import jax.numpy as jnp
from jax import lax
from jax.experimental import pallas as pl
from jax.experimental.pallas import tpu as pltpu
from jax.sharding import PartitionSpec as P

EXPERTS = 64
TOP = 8
SLOTS = 10
BF = jnp.bfloat16
F32 = jnp.float32
VMEM = pl.BlockSpec(memory_space=pltpu.VMEM)
SMEM = pl.BlockSpec(memory_space=pltpu.SMEM)
HBM = pl.BlockSpec(memory_space=pltpu.HBM)


def call(body, outs, args, places=None, scratch=(), flops=0, aliases=None, out_places=None, limit=40):
    places = places or [VMEM] * len(args)
    moved = sum(a.size * a.dtype.itemsize for a in args)
    return pl.pallas_call(
        body,
        out_shape=[jax.ShapeDtypeStruct(*o) for o in outs],
        in_specs=places,
        out_specs=out_places or [VMEM] * len(outs),
        scratch_shapes=scratch,
        input_output_aliases=aliases or {},
        compiler_params=pltpu.CompilerParams(vmem_limit_bytes=limit << 20),
        cost_estimate=pl.CostEstimate(flops=flops, bytes_accessed=moved, transcendentals=0),
    )(*args)


def iota(shape, dim):
    return lax.broadcasted_iota(jnp.int32, shape, dim)


def ones_where(condition):
    return jnp.where(condition, F32(1.0), F32(0.0)).astype(BF)


def dot(a, b):
    return jnp.dot(a, b, preferred_element_type=F32)


def pack(extra):
    n = extra.shape[0]
    shape = (4 * n, 4 * n)
    pieces = jnp.concatenate([extra[:, f * 128:(f + 1) * 128] for f in range(4)], axis=0)
    return dot(ones_where(iota(shape, 1) == (iota(shape, 0) & 3) * n + (iota(shape, 0) >> 2)), pieces).astype(BF)


def z_first(i):
    return ((i & 3) << 4) + (i >> 2)


def unpack(pieces):
    n = pieces.shape[0] // 4
    shape = (4 * n, 4 * n)
    order = ones_where(iota(shape, 0) == (iota(shape, 1) & 3) * n + (iota(shape, 1) >> 2))
    parts = dot(order, pieces).astype(BF)
    return jnp.concatenate([parts[f * n:(f + 1) * n] for f in range(4)], axis=1)


def rows_of(half):
    return jnp.concatenate([half[:, :512], unpack(half[:, 512:])], axis=0)


def select_body(c, *refs):
    ids_ref, tokens_ref, out_ref, ids_at, tokens_at, sems = refs[c:]
    copies = [
        pltpu.make_async_copy(ids_ref, ids_at, sems.at[0]),
        pltpu.make_async_copy(tokens_ref, tokens_at, sems.at[1]),
    ]
    for copy in copies:
        copy.start()
    rows = tokens_at.shape[0]
    shape, square = (EXPERTS, rows), (rows, rows)
    big = (EXPERTS * 8, EXPERTS)

    def expert(i):
        if c == 0:
            return z_first(i)
        return ((((i >> 4) + refs[0][2]) & 3) << 4) + (i & 15)

    spread = ones_where(expert(iota(big, 0) >> 3) == iota(big, 1))
    before = ones_where(iota(square, 0) < iota(square, 1))
    copies[0].wait()
    ids = ids_at[...]
    chosen = jnp.zeros(shape, F32)
    for k in range(TOP):
        chosen = chosen + jnp.where(ids[k:k + 1, :] == iota(shape, 0), F32(1.0), F32(0.0))
    slot = jnp.where(chosen > 0, dot(chosen.astype(BF), before), F32(-1.0)).astype(BF)
    wide = dot(spread, slot)
    row = iota(wide.shape, 0) & 7
    main = ones_where(wide == (row + SLOTS * c).astype(F32))
    extra = wide == ((row >> 2) + (SLOTS * c + 8)).astype(F32)
    pieces = [ones_where(extra & ((row & 3) == f)) for f in range(4)]
    copies[1].wait()
    tokens = tokens_at[...]
    out_ref[:, :512] = dot(main, tokens).astype(BF)
    total = jnp.zeros((EXPERTS * 8, 128), F32)
    for f in range(4):
        total = total + dot(pieces[f], tokens[:, f * 128:(f + 1) * 128])
    out_ref[:, 512:] = total.astype(BF)


def gate_up_body(place_ref, blocks_ref, gate_ref, up_ref, kept_ref, sent_ref, blocks_at, weights_at, total, sems):
    def copies(y):
        at = pl.ds(y * 512, 512)
        return (
            pltpu.make_async_copy(blocks_ref.at[at, :], blocks_at.at[at, :], sems.at[y, 0]),
            pltpu.make_async_copy(gate_ref.at[at, :], weights_at.at[at, pl.ds(0, 384)], sems.at[y, 1]),
            pltpu.make_async_copy(up_ref.at[at, :], weights_at.at[at, pl.ds(384, 384)], sems.at[y, 2]),
        )

    for y in range(2):
        for copy in copies(y):
            copy.start()
    first = place_ref[1] == 0
    for y in range(4):
        for copy in copies(y):
            copy.wait()
        if y < 2:
            for copy in copies(y + 2):
                copy.start()
        weights = weights_at[y * 512:(y + 1) * 512, :]
        sums = []
        for h in range(2):
            own = dot(rows_of(blocks_at[y * 512 + h * 256:y * 512 + (h + 1) * 256, :]), weights)
            sums.append(own if y == 0 else total[h * 320:(h + 1) * 320, :] + own)
        if y < 3:
            for h in range(2):
                total[h * 320:(h + 1) * 320, :] = sums[h]
        else:
            kept_ref[...] = jnp.where(first, sums[0], sums[1])
            sent_ref[...] = jnp.where(first, sums[1], sums[0]).astype(BF)


def act_body(kept_ref, got_ref, hidden_ref):
    gate = kept_ref[:, :384] + got_ref[:, :384].astype(F32)
    up = kept_ref[:, 384:] + got_ref[:, 384:].astype(F32)
    hidden_ref[...] = (gate / (1.0 + jnp.exp(-gate)) * up).astype(BF)


def down_half(side, hidden_ref, down_ref, out_ref, slab, sem):
    units = jnp.concatenate([hidden_ref[y * 320:(y + 1) * 320, :] for y in range(4)], axis=1)
    total = dot(units, down_ref[...])
    rows = total.astype(BF)
    slab[:, :512] = rows[:256]
    slab[:, 512:] = pack(rows[256:])
    copy = pltpu.make_async_copy(slab, out_ref.at[pl.ds(pl.multiple_of(side * 256, 256), 256), :], sem)
    copy.start()
    copy.wait()


def down_own_body(place_ref, hidden_ref, down_ref, out_ref, slab, sem):
    down_half(place_ref[1], hidden_ref, down_ref, out_ref, slab, sem)


def down_other_body(place_ref, hidden_ref, down_ref, own_ref, out_ref, slab, sem):
    down_half(1 - place_ref[1], hidden_ref, down_ref, out_ref, slab, sem)


def slots_of(ids):
    rows = ids.shape[0]
    shape = (rows, EXPERTS)
    chosen = jnp.zeros(shape, F32)
    for k in range(TOP):
        chosen = chosen + jnp.where(ids[:, k:k + 1] == iota(shape, 1), F32(1.0), F32(0.0))
    square = (rows, rows)
    rank = dot(ones_where(iota(square, 0) > iota(square, 1)), chosen.astype(BF))
    return chosen, jnp.where(chosen > 0, rank, F32(-1.0))


def weights_of(slot, probs, c, expert):
    high = probs.astype(BF)
    low = (probs - high.astype(F32)).astype(BF)
    shape = (EXPERTS, EXPERTS * 8)
    spread = ones_where(expert(iota(shape, 1) >> 3) == iota(shape, 0))
    wide = dot(slot.astype(BF), spread)
    row = iota(wide.shape, 1) & 7
    main = wide == (row + SLOTS * c).astype(F32)
    extra = wide == ((row >> 2) + (SLOTS * c + 8)).astype(F32)
    parts = [dot(part, spread) for part in (high, low)]
    masks = [main] + [extra & ((row & 3) == f) for f in range(4)]
    return [jnp.where(mask, part, F32(0.0)).astype(BF) for mask in masks for part in parts]


def weighted(weights, block):
    n = weights.shape[0] // 10
    main = dot(weights[:2 * n], block[:, :512])
    extra = dot(weights[2 * n:], block[:, 512:])
    pieces = [extra[2 * f * n:(2 * f + 1) * n] + extra[(2 * f + 1) * n:(2 * f + 2) * n] for f in range(4)]
    return main[:n] + main[n:] + jnp.concatenate(pieces, axis=1)


def combine_a_body(place_ref, ids_ref, logits_ref, block_ref, acc_ref, weights_ref):
    chosen, slot = slots_of(ids_ref[...])
    raised = jnp.where(chosen > 0, jnp.exp(logits_ref[...]), F32(0.0))
    probs = raised / jnp.sum(raised, axis=1, keepdims=True)

    def expert(i):
        return (((place_ref[2] + 4 - (i >> 4)) & 3) << 4) + (i & 15)

    acc_ref[...] = weighted(jnp.concatenate(weights_of(slot, probs, 0, expert), axis=0), block_ref[...])
    for i, part in enumerate(weights_of(slot, probs, 1, z_first)):
        weights_ref[i * 128:(i + 1) * 128, :] = part


def combine_b_body(acc_ref, weights_ref, block_ref, out_ref):
    out_ref[...] = (acc_ref[...] + weighted(weights_ref[...], block_ref[...])).astype(BF)


def shift(x, axis, size, by):
    return lax.ppermute(x, axis, [(i, (i + by) % size) for i in range(size)])


def exchange(x, groups):
    return lax.all_to_all(x, "ep", split_axis=0, concat_axis=0, tiled=True, axis_index_groups=groups)


WHOLE = [[z_first(i) for i in range(64)]]
ALONG_Z = [[x * 16 + z for z in range(16)] for x in range(4)]


def shift_x(part, by):
    return lax.ppermute(part, "ep", [(i, (i + 16 * by) % 64) for i in range(64)])


def out_along_x(slabs, x):
    own, one, two, three = (slabs[d * 128:(d + 1) * 128] for d in range(4))
    parts = [own, shift_x(three, 3), shift_x(two, 2), shift_x(one, 1)]
    parts = jnp.stack([p.reshape(16, 8, 640) for p in parts + parts[:3]])
    parts = lax.dynamic_slice_in_dim(parts, (4 - x) & 3, 4, 0)
    return parts.transpose(1, 0, 2, 3).reshape(512, 640)


def back_along_x(slabs, x):
    slabs = slabs.reshape(16, 4, 8, 640)
    parts = []
    for d in range(4):
        part = lax.dynamic_slice_in_dim(slabs, (x + d) & 3, 1, 1).reshape(128, 640)
        parts.append(shift_x(part, d) if d else part)
    return jnp.concatenate(parts, axis=0)


def in_hbm(x):
    return pltpu.with_memory_space_constraint(x, pltpu.HBM)


def gate_up(place, blocks, gate_w, up_w):
    return call(
        gate_up_body,
        [((320, 768), F32), ((320, 768), BF)],
        (place, in_hbm(blocks), in_hbm(gate_w), in_hbm(up_w)),
        [SMEM, HBM, HBM, HBM],
        [
            pltpu.VMEM((2048, 640), BF),
            pltpu.VMEM((2048, 768), BF),
            pltpu.VMEM((640, 768), F32),
            pltpu.SemaphoreType.DMA((4, 3)),
        ],
        1 << 31,
    )


def activate(kept, sent):
    hidden, = call(act_body, [((320, 384), BF)], (kept, shift(sent, "sec", 2, 1)))
    return hidden


def gather(hidden):
    return lax.all_gather(hidden, "tp", axis=0, tiled=True)


def contract(place, full, down_w):
    other = shift(full, "sec", 2, 1)
    out = [((512, 640), BF)]
    scratch = [pltpu.VMEM((256, 640), BF), pltpu.SemaphoreType.DMA]
    own, = call(down_own_body, out, (place, full, down_w), [SMEM, VMEM, VMEM], scratch, 1 << 29, None, [HBM])
    produced, = call(
        down_other_body, out, (place, other, down_w, own), [SMEM, VMEM, VMEM, HBM], scratch, 1 << 29, {3: 0}, [HBM]
    )
    return produced


def per_device(tokens, router_weight, expert_ids, gate_weight, up_weight, down_weight):
    x = (lax.axis_index("ep") >> 4).astype(jnp.int32)
    place = jnp.stack([lax.axis_index("tp"), lax.axis_index("sec"), x]).astype(jnp.int32)
    gate_w, up_w, down_w = gate_weight[0], up_weight[0], down_weight[0]
    names = expert_ids.T
    scratch = [pltpu.VMEM(names.shape, jnp.int32), pltpu.VMEM(tokens.shape, BF), pltpu.SemaphoreType.DMA((2,))]
    sources = (in_hbm(names), in_hbm(tokens))
    out = [((512, 640), BF)]
    slabs_a, = call(functools.partial(select_body, 0), out, sources, [HBM, HBM], scratch)
    slabs_b, = call(functools.partial(select_body, 1), out, (place, *sources), [SMEM, HBM, HBM], scratch)
    block_a = exchange(slabs_a, WHOLE)
    slabs_b = out_along_x(slabs_b, x)
    block_a, slabs_b = lax.optimization_barrier((block_a, slabs_b))
    block_b = exchange(slabs_b, ALONG_Z)

    blocks_a = lax.all_gather(block_a, "tp", axis=0, tiled=True)
    blocks_a, block_b = lax.optimization_barrier((blocks_a, block_b))
    kept_a, sent_a = gate_up(place, blocks_a, gate_w, up_w)
    blocks_b = lax.all_gather(block_b, "tp", axis=0, tiled=True)
    produced_a = contract(place, gather(activate(kept_a, sent_a)), down_w)
    blocks_b, _ = lax.optimization_barrier((blocks_b, produced_a))
    back_a = exchange(produced_a, ALONG_Z)
    produced_b = contract(place, gather(activate(*gate_up(place, blocks_b, gate_w, up_w))), down_w)
    produced_b, back_a = lax.optimization_barrier((produced_b, back_a))
    back_b = exchange(produced_b, WHOLE)
    back_a = back_along_x(back_a, x)

    logits = dot(tokens, router_weight)
    logits, _ = lax.optimization_barrier((logits, produced_b))
    logits = logits + shift(logits, "sec", 2, 1)
    logits = logits + shift(logits, "tp", 4, 1)
    logits = logits + shift(logits, "tp", 4, 2)
    acc, weights_b = call(
        combine_a_body,
        [((128, 512), F32), ((1280, 512), BF)],
        (place, expert_ids, logits, back_a),
        [SMEM] + [VMEM] * 3,
    )
    mixture, = call(combine_b_body, [((128, 512), BF)], (acc, weights_b, back_b))
    return mixture


def solution(mesh):
    placed = (
        P("ep", ("sec", "tp")),
        P(("sec", "tp"), None),
        P("ep", None),
        P("ep", "sec", "tp"),
        P("ep", "sec", "tp"),
        P("ep", None, ("sec", "tp")),
    )
    return jax.shard_map(
        per_device, mesh=mesh, in_specs=placed, out_specs=P("ep", ("sec", "tp")), check_vma=False
    )
```
